32 devices in a mesh: groups: 2 (over y), row: 4 (over x, core), col: 4 (over z).
Axes of the slice: x: 2, y: 2, z: 4, core: 2. Of those that a mesh axis runs over, the one named last changes fastest.
Arguments:
- tile_values: bfloat16 [1536, 128, 128], P(('groups', 'row', 'col')), parts along dimension 0, may hold values from 0 to 1, as said below
- tile_row: int32 [1536], P(('groups', 'row', 'col')), parts along dimension 0, may hold values from 0 to 63, as said below
- tile_column: int32 [1536], P(('groups', 'row', 'col')), parts along dimension 0, may hold values from 0 to 63, as said below
- pair_counts: int32 [8, 4], P(('groups', 'row')), parts along dimension 0, may hold values from 0 to 3, as said below
- start_block: float32 [64, 16384], P(None, ('groups', 'row', 'col')), parts along dimension 1, may hold values from -18 to 18
Outputs:
- vectors: float32 [64, 16384], P(None, ('groups', 'row', 'col')), parts along dimension 1
- vector_images: float32 [64, 16384], P(None, ('groups', 'row', 'col')), parts along dimension 1
The draws below stay inside these ranges and needn't reach their ends.
There are 2 independent parts, one for each index of `groups`. The reference program is written for one: setup_inputs(seed, part) draws one part's arguments, and reference() takes and returns one part's arrays. A program takes and returns all parts, laid end to end along the dimension named above; each array names one. Nothing has to cross between parts.
Inputs may be any that keep to these rules, and one draw needn't show every extreme that they name: `tile_row`: slot t = ((r * 4 + c) * 4 + b) * 4 * 3 + e * 3 + q holds a tile whose row lies in row block r and class e, row index r * 16 + e * 4 + u, and whose column lies in block b and class c, column index b * 16 + c * 4 + v, with u and v below 4. `tile_column`: see tile_row; the tile in slot (r, c, b, e, q) has the swapped row and column of the tile in slot (b, e, r, c, q); where r = b and c = e the slot holds a diagonal tile. `pair_counts`: Symmetric; every draw has row blocks whose pairs all hold 3. `tile_values`: the tile in slot (r, c, b, e, q) is the transpose of the one in slot (b, e, r, c, q); diagonal tiles are symmetric.
All inputs are finite; a program needn't handle non-finite values.
Results may differ from the reference program's by a relative error of at most 0.0004.
The reference program's roundings to bfloat16 on the way count: a program that leaves them out, or rounds other values in their place, can miss the bound.
Values may be sent and summed in bfloat16 or wider, within the bound.
A program may use at most 64 MiB of HBM per device.

```python
import jax
import jax.numpy as jnp
from jax import lax

K = 64
TILE = 128
TB = 16
Q = 3
ITERS = 2
FILT = 4
NTR = 64
N = 8192
CW = 4
SLOTS = 48
TILES = 768
N_ROW = 4
N_COL = 4


def slot_flags():
    block_r = jnp.arange(N_ROW)[:, None, None, None, None]
    class_c = jnp.arange(N_COL)[None, :, None, None, None]
    block_b = jnp.arange(N_ROW)[None, None, :, None, None]
    class_e = jnp.arange(N_COL)[None, None, None, :, None]
    shape_all = (N_ROW, N_COL, N_ROW, N_COL, Q)
    own_side = jnp.broadcast_to((block_r < block_b) | (block_r == block_b) & (class_c <= class_e), shape_all)
    self_pair = jnp.broadcast_to((block_r == block_b) & (class_c == class_e), shape_all)
    return (block_r, class_c, block_b, class_e, own_side, self_pair)


def pattern_tables(key):
    row_key, column_key, count_key, active_key = jax.random.split(key, 4)
    shape_all = (N_ROW, N_COL, N_ROW, N_COL, Q)
    block_r, class_c, block_b, class_e, own_side, self_pair = slot_flags()
    first_pos = jax.random.randint(row_key, shape_all, 0, CW)
    second_pos = jax.random.randint(column_key, shape_all, 0, CW)
    mirror_first = jnp.transpose(first_pos, (2, 3, 0, 1, 4))
    mirror_second = jnp.transpose(second_pos, (2, 3, 0, 1, 4))
    row_pos = jnp.where(own_side, first_pos, mirror_second)
    column_pos = jnp.where(own_side, second_pos, mirror_first)
    column_pos = jnp.where(self_pair, row_pos, column_pos)
    rows_drawn = (block_r * TB + class_e * CW + row_pos).reshape(-1).astype(jnp.int32)
    columns_drawn = (block_b * TB + class_c * CW + column_pos).reshape(-1).astype(jnp.int32)
    ordering = jax.random.permutation(active_key, N_ROW)
    active = ordering < max(1, N_ROW // 4)
    sparse_counts = jax.random.randint(count_key, (N_ROW, N_ROW), 0, 2)
    upper = jnp.arange(N_ROW)[:, None] <= jnp.arange(N_ROW)[None, :]
    sparse_counts = jnp.where(upper, sparse_counts, sparse_counts.T)
    counts_drawn = jnp.where(active[:, None] | active[None, :], Q, jnp.minimum(sparse_counts, Q)).astype(jnp.int32)
    return (rows_drawn, columns_drawn, counts_drawn)


def draw_tile_row(key, part):
    rows_drawn, columns_drawn, counts_drawn = pattern_tables(key)
    return rows_drawn


def draw_tile_column(key, part):
    rows_drawn, columns_drawn, counts_drawn = pattern_tables(key)
    return columns_drawn


def draw_pair_counts(key, part):
    rows_drawn, columns_drawn, counts_drawn = pattern_tables(key)
    return counts_drawn


def draw_tile_values(key, part):
    key = jax.random.fold_in(key, 11)
    value_key, scale_key = jax.random.split(key)
    block_r, class_c, block_b, class_e, own_side, self_pair = slot_flags()
    total_slots = N_ROW * N_COL * N_ROW * N_COL * Q
    slot_ids = jnp.arange(total_slots, dtype=jnp.int32).reshape(N_ROW, N_COL, N_ROW, N_COL, Q)
    canonical = jnp.where(own_side, slot_ids, jnp.transpose(slot_ids, (2, 3, 0, 1, 4))).reshape(-1)

    def one_tile(identity):
        entry_key = jax.random.fold_in(value_key, identity)
        level_key = jax.random.fold_in(scale_key, identity)
        entries = jax.random.uniform(entry_key, (TILE, TILE), jnp.float32, 0.05, 1.0)
        level = jnp.exp(jax.random.uniform(level_key, (), jnp.float32, jnp.log(0.1), 0.0))
        return entries * level
    values = jax.vmap(one_tile)(canonical)
    flipped = jnp.swapaxes(values, 1, 2)
    values = jnp.where(own_side.reshape(-1)[:, None, None], values, flipped)
    values = jnp.where(self_pair.reshape(-1)[:, None, None], 0.5 * (values + flipped), values)
    return values.astype(jnp.bfloat16)


def draw_start_block(key, part):
    key = jax.random.fold_in(key, 5)
    position = jnp.arange(N, dtype=jnp.float32) / N
    noise = jax.random.truncated_normal(key, -6.0, 6.0, (K, N), jnp.float32)
    return noise * (1.0 + 2.0 * position[None, :])


def setup_inputs(seed: int = 0, part: int = 0) -> dict:
    seeds = jax.random.split(jax.random.key(seed), 6)
    part_splits = jax.random.split(jax.random.fold_in(seeds[5], part), 6)
    tile_values = draw_tile_values(jax.random.fold_in(jax.random.fold_in(seeds[5], part), 71), part)
    tile_row = draw_tile_row(jax.random.fold_in(jax.random.fold_in(seeds[5], part), 71), part)
    tile_column = draw_tile_column(jax.random.fold_in(jax.random.fold_in(seeds[5], part), 71), part)
    pair_counts = draw_pair_counts(jax.random.fold_in(jax.random.fold_in(seeds[5], part), 71), part)
    start_block = draw_start_block(jax.random.fold_in(jax.random.fold_in(seeds[5], part), 71), part)
    return dict(tile_values=tile_values, tile_row=tile_row, tile_column=tile_column, pair_counts=pair_counts, start_block=start_block)


highest = lax.Precision.HIGHEST

def inner_mean(left_rows, right_rows, rows_total):
    return jnp.einsum('mn,pn->mp', left_rows, right_rows, precision=highest) / rows_total

def small_problem(gram_basis, gram_image, width_k):
    lower_factor = jnp.linalg.cholesky(gram_basis)
    symmetric = 0.5 * (gram_image + gram_image.T)
    halfway = jax.scipy.linalg.solve_triangular(lower_factor, symmetric, lower=True)
    reduced = jax.scipy.linalg.solve_triangular(lower_factor, halfway.T, lower=True)
    coords = lower_factor[:width_k, :]
    shifted = 2.5 * jnp.eye(gram_basis.shape[0], dtype=jnp.float32) - reduced
    for filtering in range(FILT):
        coords = jnp.dot(coords, shifted, precision=highest)
        factor = jnp.linalg.cholesky(jnp.dot(coords, coords.T, precision=highest))
        coords = jax.scipy.linalg.solve_triangular(factor, coords, lower=True)
    return jax.scipy.linalg.solve_triangular(lower_factor, coords.T, lower=True, trans=1).T

def operator_apply(current, degree_scale, tile_values, tile_row, tile_column, live_mask):
    scaled_panel = (current * degree_scale[None, :]).astype(jnp.bfloat16)
    column_tiles = scaled_panel.reshape(K, NTR, TILE)
    batches = TILES // SLOTS

    def accumulate(running_total, batch_index):
        offset = batch_index * SLOTS
        values = lax.dynamic_slice_in_dim(tile_values, offset, SLOTS, 0).astype(jnp.float32)
        row_index = lax.dynamic_slice_in_dim(tile_row, offset, SLOTS, 0)
        column_index = lax.dynamic_slice_in_dim(tile_column, offset, SLOTS, 0)
        weights = lax.dynamic_slice_in_dim(live_mask, offset, SLOTS, 0)
        chosen = jnp.take(column_tiles, column_index, axis=1).astype(jnp.float32)
        products = jnp.einsum('knc,nac->nka', chosen, values, precision=highest) * weights[:, None, None]
        return (running_total + jax.ops.segment_sum(products, row_index, num_segments=NTR), None)
    running_total, unused = lax.scan(accumulate, jnp.zeros((NTR, K, TILE), jnp.float32), jnp.arange(batches, dtype=jnp.int32))
    product = jnp.transpose(running_total, (1, 0, 2)).reshape(K, N)
    return current - degree_scale[None, :] * (product + degree_scale[None, :] * current)

def reference(tile_values, tile_row, tile_column, pair_counts, start_block):
    tile_index = jnp.arange(TILES, dtype=jnp.int32)
    row_block = tile_index // (N_COL * SLOTS)
    column_block = tile_index % SLOTS // (N_COL * Q)
    live_mask = (tile_index % Q < pair_counts[row_block, column_block]).astype(jnp.float32)
    row_totals = lax.optimization_barrier(jnp.sum(tile_values, axis=2, dtype=jnp.float32)) * live_mask[:, None]
    degree = 1.0 + jax.ops.segment_sum(row_totals, tile_row, num_segments=NTR).reshape(N)
    degree_scale = 1.0 / jnp.sqrt(degree)

    def apply_operator(current):
        return operator_apply(current, degree_scale, tile_values, tile_row, tile_column, live_mask)
    lower_start = jnp.linalg.cholesky(inner_mean(start_block, start_block, N))
    current = jax.scipy.linalg.solve_triangular(lower_start, start_block, lower=True)
    imaged = apply_operator(current)
    previous = current
    previous_image = imaged
    for iteration in range(ITERS):
        rayleigh = inner_mean(current, imaged, N)
        residual = imaged - jnp.dot(0.5 * (rayleigh + rayleigh.T), current, precision=highest)
        residual_image = apply_operator(residual)
        if iteration == 0:
            basis_rows = jnp.concatenate([current, residual], axis=0)
            images = jnp.concatenate([imaged, residual_image], axis=0)
        else:
            basis_rows = jnp.concatenate([current, residual, previous], axis=0)
            images = jnp.concatenate([imaged, residual_image, previous_image], axis=0)
        gram_basis = inner_mean(basis_rows, basis_rows, N)
        gram_image = inner_mean(basis_rows, images, N)
        coefficients = small_problem(gram_basis, gram_image, K)
        tail_coef = coefficients[:, K:]
        current = jnp.dot(coefficients, basis_rows, precision=highest)
        imaged = jnp.dot(coefficients, images, precision=highest)
        previous = jnp.dot(tail_coef, basis_rows[K:], precision=highest)
        previous_image = jnp.dot(tail_coef, images[K:], precision=highest)
    return (current, imaged)
```

```python
import functools

import jax
import jax.numpy as jnp
from jax import lax
from jax.experimental import pallas as pl
from jax.experimental.pallas import tpu as pltpu
from jax.sharding import PartitionSpec as P

Q = 3
TILE = 128
MESH = pl.DeviceIdType.MESH
highest = lax.Precision.HIGHEST
f32 = jnp.float32


def mm(left, right):
    return jnp.dot(left, right, precision=highest, preferred_element_type=f32)


def mt(left, right):
    return lax.dot_general(
        left, right, (((1,), (1,)), ((), ())), precision=highest, preferred_element_type=f32
    )


def eye(rows, columns=None):
    columns = rows if columns is None else columns
    shape = (rows, columns)
    return (
        lax.broadcasted_iota(jnp.int32, shape, 0) == lax.broadcasted_iota(jnp.int32, shape, 1)
    ).astype(f32)


def factor_inverse(matrix):
    width = matrix.shape[0]
    work = jnp.concatenate([matrix, eye(width)], axis=1)
    row_id = lax.broadcasted_iota(jnp.int32, (width, 1), 0)
    for j in range(width - 1):
        pivot = work[j : j + 1, :]
        column = work[:, j : j + 1]
        scaled = jnp.where(row_id > j, column * (1.0 / pivot[:, j : j + 1]), 0.0)
        work = work - scaled * pivot
    diagonal = jnp.sum(work[:, :width] * eye(width), axis=1, keepdims=True)
    return work[:, width:] * lax.rsqrt(diagonal)


def filtered(reduced, width_k):
    size = reduced.shape[0]
    shifted = 2.5 * eye(size) - reduced
    coords = mm(shifted[:width_k], shifted)
    coords = mm(factor_inverse(mt(coords, coords)), coords)
    coords = mm(mm(coords, shifted), shifted)
    return mm(factor_inverse(mt(coords, coords)), coords)


def sym(matrix):
    return 0.5 * (matrix + matrix.T)


def kernel(
    sizes,
    tiles,
    spots,
    start,
    current_out,
    imaged_out,
    panels,
    sums,
    arrived,
    degree_sums,
    degree_arrived,
    *rest,
):
    rows, columns, width_k, class_tiles, rows_total = sizes
    devices = rows * columns
    ar_bufs, sems = rest[:12], rest[12:]
    my_row, my_col = lax.axis_index("row"), lax.axis_index("col")
    me = my_row * columns + my_col
    own = class_tiles * TILE
    flat = devices <= 16

    def peer_flat(step):
        other = lax.rem(me + step, devices)
        return {"row": other // columns, "col": lax.rem(other, columns)}

    barrier = pltpu.get_barrier_semaphore()
    if flat:
        for step in range(1, devices):
            pl.semaphore_signal(barrier, inc=1, device_id=peer_flat(step), device_id_type=MESH)
        pl.semaphore_wait(barrier, devices - 1)
    else:
        for step in range(1, rows):
            pl.semaphore_signal(
                barrier, inc=1, device_id={"row": lax.rem(my_row + step, rows)}, device_id_type=MESH
            )
        for step in range(1, columns):
            pl.semaphore_signal(
                barrier,
                inc=1,
                device_id={"col": lax.rem(my_col + step, columns)},
                device_id_type=MESH,
            )
        pl.semaphore_wait(barrier, rows + columns - 2)

    def send(source, target, send_sem, recv_sem, device):
        copy = pltpu.make_async_remote_copy(
            src_ref=source,
            dst_ref=target,
            send_sem=send_sem,
            recv_sem=recv_sem,
            device_id=device,
            device_id_type=MESH,
        )
        copy.start()
        return copy

    def total_start(stage, value):
        source, landed, result = ar_bufs[3 * stage : 3 * stage + 3]
        sem = sems[stage]
        if not flat:
            source[...] = value
            return [
                send(
                    source,
                    landed.at[my_col],
                    sem.at[0, step],
                    sem.at[1, step],
                    {"col": lax.rem(my_col + step, columns)},
                )
                for step in range(1, columns)
            ]
        piece = width_k // devices
        for i in range(devices):
            source[i] = value[i * piece : (i + 1) * piece]
        return [
            send(
                source.at[lax.rem(me + step, devices)],
                landed.at[step],
                sem.at[0, step],
                sem.at[1, step],
                peer_flat(step),
            )
            for step in range(1, devices)
        ]

    def total_finish(stage, copies):
        source, landed, result = ar_bufs[3 * stage : 3 * stage + 3]
        sem = sems[stage]
        if not flat:
            landed[my_col] = source[...]
            for copy in copies:
                copy.wait()
            value = landed[0]
            for i in range(1, columns):
                value = value + landed[i]
            result[my_row] = value
            copies = [
                send(
                    result.at[my_row],
                    result.at[my_row],
                    sem.at[2, step],
                    sem.at[3, step],
                    {"row": lax.rem(my_row + step, rows)},
                )
                for step in range(1, rows)
            ]
            for copy in copies:
                copy.wait()
            value = result[0]
            for i in range(1, rows):
                value = value + result[i]
            return value
        value = source[me]
        for step, copy in enumerate(copies):
            copy.wait_recv()
            value = value + landed[step + 1]
        result[me] = value
        second = [
            send(
                result.at[me], result.at[me], sem.at[2, step], sem.at[3, step], peer_flat(step)
            )
            for step in range(1, devices)
        ]
        for copy in copies:
            copy.wait_send()
        for copy in second:
            copy.wait()
        return jnp.concatenate([result[i] for i in range(devices)], axis=0)

    def total(stage, value):
        return total_finish(stage, total_start(stage, value))

    def sum_start(source, target, sem):
        return [
            send(
                source.at[lax.rem(my_row + step, rows)],
                target.at[step],
                sem.at[0, step],
                sem.at[1, step],
                {"row": lax.rem(my_row + step, rows)},
            )
            for step in range(1, rows)
        ]

    def sum_finish(source, target, copies):
        value = source[my_row]
        for step, copy in enumerate(copies):
            copy.wait()
            value = value + target[step + 1]
        return jnp.concatenate([value[v] for v in range(class_tiles)], axis=1)

    inverse_total = 1.0 / rows_total
    start_copies = total_start(0, mt(start[...], start[...]) * inverse_total)

    degree_sums[...] = jnp.zeros_like(degree_sums)
    ones = jnp.ones((16, TILE), jnp.bfloat16)

    def degree_step(pair, carry):
        block, group = pair // columns, lax.rem(pair, columns)
        for q in range(Q):
            slot = pair * Q + q
            part = jnp.dot(ones, tiles[slot], preferred_element_type=f32)[:8]
            for v in range(class_tiles):
                degree_sums[block, v] += part * spots[slot * (class_tiles + 1) + 1 + v].astype(f32)
        return carry

    lax.fori_loop(0, rows * columns, degree_step, 0)
    degree_copies = sum_start(degree_sums, degree_arrived, sems[4])
    current = mm(factor_inverse(total_finish(0, start_copies)), start[...])
    degree = 1.0 + sum_finish(degree_sums, degree_arrived, degree_copies)[:1]
    scale = 1.0 / jnp.sqrt(degree)

    def operate(stage, value):
        panel_ref, sum_ref, arrived_ref = panels.at[stage], sums.at[stage], arrived.at[stage]
        gather_sem, sum_sem = sems[5 + 2 * stage], sems[6 + 2 * stage]
        panel = (value * scale).astype(jnp.bfloat16)
        for v in range(class_tiles):
            panel_ref[my_col, v] = panel[:, v * TILE : (v + 1) * TILE]
        copies = [
            send(
                panel_ref.at[my_col],
                panel_ref.at[my_col],
                gather_sem.at[0, step],
                gather_sem.at[1, step],
                {"col": lax.rem(my_col + step, columns)},
            )
            for step in range(1, columns)
        ]
        sum_ref[...] = jnp.zeros_like(sum_ref)
        for step in range(columns):
            if step:
                copies[step - 1].wait_recv()
            group = lax.rem(my_col + columns - step, columns)

            def block_step(block, carry):
                for q in range(Q):
                    slot = (block * columns + group) * Q + q
                    base = slot * (class_tiles + 1)
                    chosen = panel_ref[group, 0]
                    for u in range(1, class_tiles):
                        chosen = jnp.where(spots[base] == u, panel_ref[group, u], chosen)
                    part = jnp.dot(chosen, tiles[slot], preferred_element_type=f32)
                    for v in range(class_tiles):
                        sum_ref[block, v] += part * spots[base + 1 + v].astype(f32)
                return carry

            lax.fori_loop(0, rows, block_step, 0)
        for copy in copies:
            copy.wait_send()
        summed = sum_finish(sum_ref, arrived_ref, sum_start(sum_ref, arrived_ref, sum_sem))
        return value - scale * (summed + scale * value)

    k = width_k
    imaged = operate(0, current)
    rayleigh = sym(total(1, mt(current, imaged) * inverse_total))
    residual = imaged - mm(rayleigh, current)
    residual_image = operate(1, residual)
    local = jnp.concatenate(
        [
            mt(residual, jnp.concatenate([current, residual], axis=0)),
            mt(residual, jnp.concatenate([imaged, residual_image], axis=0)),
            mt(current, jnp.concatenate([residual_image, residual_image], axis=0)),
        ],
        axis=1,
    )
    sent = total(2, local * inverse_total)
    g21, g22 = sent[:, :k], sent[:, k : 2 * k]
    h21 = 0.5 * (sent[:, 2 * k : 3 * k] + sent[:, 4 * k : 5 * k].T)
    h22 = sym(sent[:, 3 * k : 4 * k])
    gram = jnp.concatenate(
        [
            jnp.concatenate([eye(k), g21.T], axis=1),
            jnp.concatenate([g21, g22], axis=1),
        ],
        axis=0,
    )
    hmat = jnp.concatenate(
        [
            jnp.concatenate([rayleigh, h21.T], axis=1),
            jnp.concatenate([h21, h22], axis=1),
        ],
        axis=0,
    )
    w22 = factor_inverse(g22 - mt(g21, g21))
    w21 = -mm(w22, g21)
    inverse = jnp.concatenate(
        [eye(k, 2 * k), jnp.concatenate([w21, w22], axis=1)], axis=0
    )
    coefficients = mm(filtered(mt(mm(inverse, hmat), inverse), k), inverse)
    basis = jnp.concatenate([current, residual], axis=0)
    images = jnp.concatenate([imaged, residual_image], axis=0)
    tail = coefficients[:, k:]
    current, imaged = mm(coefficients, basis), mm(coefficients, images)
    previous, previous_image = mm(tail, residual), mm(tail, residual_image)
    from_left = mm(coefficients, hmat)
    rayleigh = sym(mt(from_left, coefficients))
    h31 = mt(from_left[:, k:], tail).T
    h33 = sym(mt(mm(tail, h22), tail))
    g31 = mt(mm(coefficients, gram)[:, k:], tail).T
    g33 = sym(mt(mm(tail, g22), tail))

    residual = imaged - mm(rayleigh, current)
    residual_image = operate(2, residual)
    local = jnp.concatenate(
        [
            mt(residual, jnp.concatenate([current, residual], axis=0)),
            mt(residual, jnp.concatenate([imaged, residual_image], axis=0)),
            mt(residual, jnp.concatenate([previous, previous_image], axis=0)),
            mt(residual_image, jnp.concatenate([current, previous], axis=0)),
        ],
        axis=1,
    )
    sent = total(3, local * inverse_total)
    g21, g22 = sent[:, :k], sent[:, k : 2 * k]
    h21 = 0.5 * (sent[:, 2 * k : 3 * k] + sent[:, 6 * k : 7 * k])
    h22 = sym(sent[:, 3 * k : 4 * k])
    g32 = sent[:, 4 * k : 5 * k].T
    h32 = 0.5 * (sent[:, 5 * k : 6 * k] + sent[:, 7 * k : 8 * k]).T
    w22 = factor_inverse(g22 - mt(g21, g21))
    l32 = mt(g32 - mt(g31, g21), w22)
    w33 = factor_inverse(g33 - mt(g31, g31) - mt(l32, l32))
    w21 = -mm(w22, g21)
    w31 = -mm(w33, g31 + mm(l32, w21))
    w32 = -mm(w33, mm(l32, w22))
    hmat = jnp.concatenate(
        [
            jnp.concatenate([rayleigh, h21.T, h31.T], axis=1),
            jnp.concatenate([h21, h22, h32.T], axis=1),
            jnp.concatenate([h31, h32, h33], axis=1),
        ],
        axis=0,
    )
    inverse = jnp.concatenate(
        [
            eye(k, 3 * k),
            jnp.concatenate([w21, w22, jnp.zeros((k, k), f32)], axis=1),
            jnp.concatenate([w31, w32, w33], axis=1),
        ],
        axis=0,
    )
    coefficients = mm(filtered(mt(mm(inverse, hmat), inverse), k), inverse)
    current_out[...] = mm(coefficients, jnp.concatenate([current, residual, previous], axis=0))
    imaged_out[...] = mm(
        coefficients, jnp.concatenate([imaged, residual_image, previous_image], axis=0)
    )


def on_device(tile_values, tile_row, tile_column, pair_counts, start_block):
    columns, rows = lax.axis_size("col"), lax.axis_size("row")
    width_k, own = start_block.shape
    class_tiles = own // TILE
    devices = rows * columns
    slots = tile_values.shape[0]
    live = jnp.arange(Q, dtype=jnp.int32)[None, :] < pair_counts[0][:, None]
    live = jnp.broadcast_to(live[:, None, :], (rows, columns, Q)).reshape(slots)
    here = (tile_column % class_tiles)[:, None] == jnp.arange(class_tiles, dtype=jnp.int32)
    spots = jnp.concatenate(
        [(tile_row % class_tiles)[:, None], (here & live[:, None]).astype(jnp.int32)], axis=1
    ).reshape(-1)
    sizes = (rows, columns, width_k, class_tiles, own * devices)
    flat = devices <= 16
    scratch = [
        pltpu.VMEM((3, columns, class_tiles, width_k, TILE), jnp.bfloat16),
        pltpu.VMEM((3, rows, class_tiles, width_k, TILE), f32),
        pltpu.VMEM((3, rows, class_tiles, width_k, TILE), f32),
        pltpu.VMEM((rows, class_tiles, 8, TILE), f32),
        pltpu.VMEM((rows, class_tiles, 8, TILE), f32),
    ]
    for width in (width_k, width_k, 6 * width_k, 8 * width_k):
        if flat:
            scratch += [pltpu.VMEM((devices, width_k // devices, width), f32)] * 3
        else:
            scratch += [
                pltpu.VMEM((width_k, width), f32),
                pltpu.VMEM((columns, width_k, width), f32),
                pltpu.VMEM((rows, width_k, width), f32),
            ]
    most = devices if flat else max(rows, columns)
    scratch += [pltpu.SemaphoreType.DMA((4, most))] * 4
    scratch += [pltpu.SemaphoreType.DMA((2, rows))]
    for stage in range(3):
        scratch += [pltpu.SemaphoreType.DMA((2, columns)), pltpu.SemaphoreType.DMA((2, rows))]
    vmem = pl.BlockSpec(memory_space=pltpu.VMEM)
    return pl.pallas_call(
        functools.partial(kernel, sizes),
        out_shape=(
            jax.ShapeDtypeStruct((width_k, own), f32),
            jax.ShapeDtypeStruct((width_k, own), f32),
        ),
        in_specs=[vmem, pl.BlockSpec(memory_space=pltpu.SMEM), vmem],
        out_specs=(vmem, vmem),
        scratch_shapes=scratch,
        compiler_params=pltpu.CompilerParams(
            collective_id=0, has_side_effects=True, vmem_limit_bytes=52 * 1024 * 1024
        ),
    )(tile_values, spots, start_block)


def solution(mesh):
    split = ("groups", "row", "col")
    placed = (P(split, None, None), P(split), P(split), P(("groups", "row"), None), P(None, split))
    return jax.shard_map(
        on_device,
        mesh=mesh,
        in_specs=placed,
        out_specs=(P(None, split), P(None, split)),
        check_vma=False,
    )
```

```python
import functools

import jax
import jax.numpy as jnp
from jax import lax
from jax.experimental import pallas as pl
from jax.experimental.pallas import tpu as pltpu
from jax.sharding import PartitionSpec as P

Q = 3
TILE = 128
PIVOTS = 8
HALVES = 2
MESH = pl.DeviceIdType.MESH
highest = lax.Precision.HIGHEST
f32 = jnp.float32


def mm(left, right):
    return jnp.dot(left, right, precision=highest, preferred_element_type=f32)


def mt(left, right):
    return lax.dot_general(
        left, right, (((1,), (1,)), ((), ())), precision=highest, preferred_element_type=f32
    )


def eye(rows, columns=None):
    columns = rows if columns is None else columns
    shape = (rows, columns)
    return (
        lax.broadcasted_iota(jnp.int32, shape, 0) == lax.broadcasted_iota(jnp.int32, shape, 1)
    ).astype(f32)


def factor_inverse(matrix):
    width = matrix.shape[0]
    lanes = 2 * width
    groups = width // 8
    work = jnp.concatenate([matrix, eye(width)], axis=1).reshape(groups, 8, lanes)
    shape = (groups, 8, lanes)
    row_id = 8 * lax.broadcasted_iota(jnp.int32, shape, 0) + lax.broadcasted_iota(
        jnp.int32, shape, 1
    )
    for first in range(0, width, PIVOTS):
        pivots, columns, entries = [], [], []
        for i in range(PIVOTS):
            j = first + i
            pivots.append(jnp.broadcast_to(work[j // 8, j % 8 : j % 8 + 1], (8, lanes)))
            columns.append(jnp.broadcast_to(work[:, :, j : j + 1], shape))
            entries.append(
                [
                    jnp.broadcast_to(pivots[i][:, first + m : first + m + 1], (8, lanes))
                    for m in range(i + 1)
                ]
            )
        for i in range(PIVOTS):
            recip = 1.0 / entries[i][i]
            scaled = jnp.where(row_id > first + i, columns[i] * recip[None], 0.0)
            work = work - scaled * pivots[i][None]
            ratios = [None] * PIVOTS
            for m in range(i + 1, PIVOTS):
                ratios[m] = entries[m][i] * recip
            for m in range(i + 1, PIVOTS):
                pivots[m] = pivots[m] - ratios[m] * pivots[i]
                columns[m] = columns[m] - ratios[m][None] * columns[i]
                for n in range(i + 1, m + 1):
                    entries[m][n] = entries[m][n] - ratios[m] * entries[n][i]
    work = work.reshape(width, lanes)
    diagonal = jnp.sum(work[:, :width] * eye(width), axis=1, keepdims=True)
    return work[:, width:] * lax.rsqrt(diagonal)


def filtered(reduced, width_k):
    size = reduced.shape[0]
    shifted = 2.5 * eye(size) - reduced
    coords = mm(shifted[:width_k], shifted)
    coords = mm(factor_inverse(mt(coords, coords)), coords)
    coords = mm(mm(coords, shifted), shifted)
    return mm(factor_inverse(mt(coords, coords)), coords)


def sym(matrix):
    return 0.5 * (matrix + matrix.T)


def kernel(
    sizes,
    tiles,
    tile_rows,
    tile_columns,
    counts,
    start,
    current_out,
    imaged_out,
    panels,
    sums,
    arrived,
    degree_sums,
    degree_arrived,
    *rest,
):
    rows, columns, width_k, class_tiles, rows_total = sizes
    devices = rows * columns
    ar_bufs, sems = rest[:18], rest[18:]
    my_row, my_col = lax.axis_index("row"), lax.axis_index("col")
    me = my_row * columns + my_col
    own = class_tiles * TILE
    flat = devices <= 16

    def peer_flat(step):
        other = lax.rem(me + step, devices)
        return {"row": other // columns, "col": lax.rem(other, columns)}

    barrier = pltpu.get_barrier_semaphore()
    if flat:
        for step in range(1, devices):
            pl.semaphore_signal(barrier, inc=1, device_id=peer_flat(step), device_id_type=MESH)
        pl.semaphore_wait(barrier, devices - 1)
    else:
        for step in range(1, rows):
            pl.semaphore_signal(
                barrier, inc=1, device_id={"row": lax.rem(my_row + step, rows)}, device_id_type=MESH
            )
        for step in range(1, columns):
            pl.semaphore_signal(
                barrier,
                inc=1,
                device_id={"col": lax.rem(my_col + step, columns)},
                device_id_type=MESH,
            )
        pl.semaphore_wait(barrier, rows + columns - 2)

    def send(source, target, send_sem, recv_sem, device):
        copy = pltpu.make_async_remote_copy(
            src_ref=source,
            dst_ref=target,
            send_sem=send_sem,
            recv_sem=recv_sem,
            device_id=device,
            device_id_type=MESH,
        )
        copy.start()
        return copy

    def total_start(stage, value):
        source, landed, result = ar_bufs[3 * stage : 3 * stage + 3]
        sem = sems[stage]
        if not flat:
            source[...] = value
            return [
                send(
                    source,
                    landed.at[my_col],
                    sem.at[0, step],
                    sem.at[1, step],
                    {"col": lax.rem(my_col + step, columns)},
                )
                for step in range(1, columns)
            ]
        piece = width_k // devices
        for i in range(devices):
            source[i] = value[i * piece : (i + 1) * piece]
        return [
            send(
                source.at[lax.rem(me + step, devices)],
                landed.at[step],
                sem.at[0, step],
                sem.at[1, step],
                peer_flat(step),
            )
            for step in range(1, devices)
        ]

    def total_finish(stage, copies):
        source, landed, result = ar_bufs[3 * stage : 3 * stage + 3]
        sem = sems[stage]
        if not flat:
            landed[my_col] = source[...]
            for copy in copies:
                copy.wait()
            value = landed[0]
            for i in range(1, columns):
                value = value + landed[i]
            result[my_row] = value
            copies = [
                send(
                    result.at[my_row],
                    result.at[my_row],
                    sem.at[2, step],
                    sem.at[3, step],
                    {"row": lax.rem(my_row + step, rows)},
                )
                for step in range(1, rows)
            ]
            for copy in copies:
                copy.wait()
            value = result[0]
            for i in range(1, rows):
                value = value + result[i]
            return value
        value = source[me]
        for step, copy in enumerate(copies):
            copy.wait_recv()
            value = value + landed[step + 1]
        result[me] = value
        second = [
            send(
                result.at[me], result.at[me], sem.at[2, step], sem.at[3, step], peer_flat(step)
            )
            for step in range(1, devices)
        ]
        for copy in copies:
            copy.wait_send()
        for copy in second:
            copy.wait()
        return jnp.concatenate([result[i] for i in range(devices)], axis=0)

    def total(stage, value):
        return total_finish(stage, total_start(stage, value))

    def sum_start(source, target, sem):
        return [
            send(
                source.at[lax.rem(my_row + step, rows)],
                target.at[step],
                sem.at[0, step],
                sem.at[1, step],
                {"row": lax.rem(my_row + step, rows)},
            )
            for step in range(1, rows)
        ]

    def sum_finish(source, target, copies):
        value = source[my_row]
        for step, copy in enumerate(copies):
            copy.wait()
            value = value + target[step + 1]
        return jnp.concatenate([value[v] for v in range(class_tiles)], axis=1)

    def weights(slot, block, q):
        place = lax.rem(tile_columns[slot], class_tiles)
        live = counts[0, block] > q
        return [
            jnp.where(jnp.logical_and(live, place == v), 1.0, 0.0).astype(f32)
            for v in range(class_tiles)
        ]

    inverse_total = 1.0 / rows_total
    start_copies = total_start(0, mt(start[...], start[...]) * inverse_total)

    degree_sums[...] = jnp.zeros_like(degree_sums)
    ones = jnp.ones((16, TILE), jnp.bfloat16)

    def degree_step(pair, carry):
        block, group = pair // columns, lax.rem(pair, columns)
        for q in range(Q):
            slot = pair * Q + q
            part = jnp.dot(ones, tiles[slot], preferred_element_type=f32)[:8]
            for v, weight in enumerate(weights(slot, block, q)):
                degree_sums[block, v] += part * weight
        return carry

    lax.fori_loop(0, rows * columns, degree_step, 0)
    degree_copies = sum_start(degree_sums, degree_arrived, sems[6])
    current = mm(factor_inverse(total_finish(0, start_copies)), start[...])
    degree = 1.0 + sum_finish(degree_sums, degree_arrived, degree_copies)[:1]
    scale = 1.0 / jnp.sqrt(degree)

    half = width_k // HALVES

    def operate(stage, value, early=None, late=None):
        panel = (value * scale).astype(jnp.bfloat16)
        gathers = []
        for h in range(HALVES):
            panel_ref, sem = panels.at[stage, h], sems[7 + 2 * (HALVES * stage + h)]
            for v in range(class_tiles):
                panel_ref[my_col, v] = panel[
                    h * half : (h + 1) * half, v * TILE : (v + 1) * TILE
                ]
            gathers.append(
                [
                    send(
                        panel_ref.at[my_col],
                        panel_ref.at[my_col],
                        sem.at[0, step],
                        sem.at[1, step],
                        {"col": lax.rem(my_col + step, columns)},
                    )
                    for step in range(1, columns)
                ]
            )
        begun = early() if early else None
        sent_sums = []
        for h in range(HALVES):
            panel_ref, sum_ref = panels.at[stage, h], sums.at[stage, h]
            sum_ref[...] = jnp.zeros_like(sum_ref)
            for step in range(columns):
                if step:
                    gathers[h][step - 1].wait_recv()
                group = lax.rem(my_col + columns - step, columns)

                def block_step(block, carry):
                    for q in range(Q):
                        slot = (block * columns + group) * Q + q
                        place = lax.rem(tile_rows[slot], class_tiles)
                        chosen = panel_ref[group, 0]
                        for u in range(1, class_tiles):
                            chosen = jnp.where(place == u, panel_ref[group, u], chosen)
                        part = jnp.dot(chosen, tiles[slot], preferred_element_type=f32)
                        for v, weight in enumerate(weights(slot, block, q)):
                            sum_ref[block, v] += part * weight
                    return carry

                lax.fori_loop(0, rows, block_step, 0)
            sum_sem = sems[8 + 2 * (HALVES * stage + h)]
            sent_sums.append(sum_start(sum_ref, arrived.at[stage, h], sum_sem))
        ended = late(begun) if late else None
        for copies in gathers:
            for copy in copies:
                copy.wait_send()
        summed = jnp.concatenate(
            [
                sum_finish(sums.at[stage, h], arrived.at[stage, h], sent_sums[h])
                for h in range(HALVES)
            ],
            axis=0,
        )
        return value - scale * (summed + scale * value), ended

    k = width_k
    imaged, _ = operate(0, current)
    rayleigh = sym(total(1, mt(current, imaged) * inverse_total))
    residual = imaged - mm(rayleigh, current)

    def begin_first():
        rows_here = jnp.concatenate([current, residual, imaged], axis=0)
        return total_start(2, mt(residual, rows_here) * inverse_total)

    def end_first(copies):
        known = total_finish(2, copies)
        g21 = known[:, :k]
        return known, factor_inverse(known[:, k : 2 * k] - mt(g21, g21))

    residual_image, (known, w22) = operate(1, residual, begin_first, end_first)
    sent = total(
        3, mt(residual_image, jnp.concatenate([residual, current], axis=0)) * inverse_total
    )
    g21, g22 = known[:, :k], known[:, k : 2 * k]
    h21 = 0.5 * (known[:, 2 * k :] + sent[:, k:])
    h22 = sym(sent[:, :k])
    gram = jnp.concatenate(
        [
            jnp.concatenate([eye(k), g21.T], axis=1),
            jnp.concatenate([g21, g22], axis=1),
        ],
        axis=0,
    )
    hmat = jnp.concatenate(
        [
            jnp.concatenate([rayleigh, h21.T], axis=1),
            jnp.concatenate([h21, h22], axis=1),
        ],
        axis=0,
    )
    w21 = -mm(w22, g21)
    inverse = jnp.concatenate(
        [eye(k, 2 * k), jnp.concatenate([w21, w22], axis=1)], axis=0
    )
    coefficients = mm(filtered(mt(mm(inverse, hmat), inverse), k), inverse)
    basis = jnp.concatenate([current, residual], axis=0)
    images = jnp.concatenate([imaged, residual_image], axis=0)
    tail = coefficients[:, k:]
    current, imaged = mm(coefficients, basis), mm(coefficients, images)
    previous, previous_image = mm(tail, residual), mm(tail, residual_image)
    from_left = mm(coefficients, hmat)
    rayleigh = sym(mt(from_left, coefficients))
    h31 = mt(from_left[:, k:], tail).T
    h33 = sym(mt(mm(tail, h22), tail))
    g31 = mt(mm(coefficients, gram)[:, k:], tail).T
    g33 = sym(mt(mm(tail, g22), tail))

    residual = imaged - mm(rayleigh, current)

    def begin_second():
        rows_here = jnp.concatenate([current, residual, imaged, previous, previous_image], axis=0)
        return total_start(4, mt(residual, rows_here) * inverse_total)

    def end_second(copies):
        known = total_finish(4, copies)
        g21, g32 = known[:, :k], known[:, 3 * k : 4 * k].T
        w22 = factor_inverse(known[:, k : 2 * k] - mt(g21, g21))
        l32 = mt(g32 - mt(g31, g21), w22)
        return known, w22, l32, factor_inverse(g33 - mt(g31, g31) - mt(l32, l32))

    residual_image, (known, w22, l32, w33) = operate(2, residual, begin_second, end_second)
    sent = total(
        5,
        mt(residual_image, jnp.concatenate([residual, current, previous], axis=0))
        * inverse_total,
    )
    g21 = known[:, :k]
    h21 = 0.5 * (known[:, 2 * k : 3 * k] + sent[:, k : 2 * k])
    h22 = sym(sent[:, :k])
    h32 = 0.5 * (known[:, 4 * k :] + sent[:, 2 * k :]).T
    w21 = -mm(w22, g21)
    w31 = -mm(w33, g31 + mm(l32, w21))
    w32 = -mm(w33, mm(l32, w22))
    hmat = jnp.concatenate(
        [
            jnp.concatenate([rayleigh, h21.T, h31.T], axis=1),
            jnp.concatenate([h21, h22, h32.T], axis=1),
            jnp.concatenate([h31, h32, h33], axis=1),
        ],
        axis=0,
    )
    inverse = jnp.concatenate(
        [
            eye(k, 3 * k),
            jnp.concatenate([w21, w22, jnp.zeros((k, k), f32)], axis=1),
            jnp.concatenate([w31, w32, w33], axis=1),
        ],
        axis=0,
    )
    coefficients = mm(filtered(mt(mm(inverse, hmat), inverse), k), inverse)
    current_out[...] = mm(coefficients, jnp.concatenate([current, residual, previous], axis=0))
    imaged_out[...] = mm(
        coefficients, jnp.concatenate([imaged, residual_image, previous_image], axis=0)
    )


def on_device(tile_values, tile_row, tile_column, pair_counts, start_block):
    columns, rows = lax.axis_size("col"), lax.axis_size("row")
    width_k, own = start_block.shape
    class_tiles = own // TILE
    devices = rows * columns
    sizes = (rows, columns, width_k, class_tiles, own * devices)
    flat = devices <= 16
    half = width_k // HALVES
    scratch = [
        pltpu.VMEM((3, HALVES, columns, class_tiles, half, TILE), jnp.bfloat16),
        pltpu.VMEM((3, HALVES, rows, class_tiles, half, TILE), f32),
        pltpu.VMEM((3, HALVES, rows, class_tiles, half, TILE), f32),
        pltpu.VMEM((rows, class_tiles, 8, TILE), f32),
        pltpu.VMEM((rows, class_tiles, 8, TILE), f32),
    ]
    for blocks in (1, 1, 3, 2, 5, 3):
        width = blocks * width_k
        if flat:
            scratch += [pltpu.VMEM((devices, width_k // devices, width), f32)] * 3
        else:
            scratch += [
                pltpu.VMEM((width_k, width), f32),
                pltpu.VMEM((columns, width_k, width), f32),
                pltpu.VMEM((rows, width_k, width), f32),
            ]
    most = devices if flat else max(rows, columns)
    scratch += [pltpu.SemaphoreType.DMA((4, most))] * 6
    scratch += [pltpu.SemaphoreType.DMA((2, rows))]
    for part in range(3 * HALVES):
        scratch += [pltpu.SemaphoreType.DMA((2, columns)), pltpu.SemaphoreType.DMA((2, rows))]
    vmem = pl.BlockSpec(memory_space=pltpu.VMEM)
    smem = pl.BlockSpec(memory_space=pltpu.SMEM)
    return pl.pallas_call(
        functools.partial(kernel, sizes),
        out_shape=(
            jax.ShapeDtypeStruct((width_k, own), f32),
            jax.ShapeDtypeStruct((width_k, own), f32),
        ),
        in_specs=[vmem, smem, smem, smem, vmem],
        out_specs=(vmem, vmem),
        scratch_shapes=scratch,
        compiler_params=pltpu.CompilerParams(
            collective_id=0, has_side_effects=True, vmem_limit_bytes=52 * 1024 * 1024
        ),
    )(tile_values, tile_row, tile_column, pair_counts, start_block)


def solution(mesh):
    split = ("groups", "row", "col")
    placed = (P(split, None, None), P(split), P(split), P(("groups", "row"), None), P(None, split))
    return jax.shard_map(
        on_device,
        mesh=mesh,
        in_specs=placed,
        out_specs=(P(None, split), P(None, split)),
        check_vma=False,
    )
```
